32 devices in a mesh: ctx: 16 (over z, y, core), head: 2 (over x).
Axes of the slice: x: 2, y: 2, z: 4, core: 2. Of those that a mesh axis runs over, the one named last changes fastest.
Arguments:
- queries: bfloat16 [12288, 2048], P('ctx', 'head')
- keys: bfloat16 [12288, 2048], P('ctx', 'head')
- values: bfloat16 [12288, 2048], P('ctx', 'head'), may hold values from -6 to 6
- w_out: bfloat16 [2048, 2048], P('head'), may hold values from -2.5 to 2.5
Outputs:
- layer_out: bfloat16 [12288, 2048], P('ctx', 'head')
The draws below stay inside these ranges and needn't reach their ends.
All inputs are finite; a program needn't handle non-finite values.
Results may differ from the reference program's by a relative error of at most 0.0067.
Values may be sent and summed in bfloat16 or wider, within the bound.
No kernel may reach another device: no remote copies, remote signals or barrier semaphores. Data moves between devices by JAX's collectives and lax.ppermute only.
A program may use at most 64 MiB of HBM per device.

```python
import math
import jax
import jax.numpy as jnp
from jax import lax

D = 2048
H = 16
HD = 128
BLOCK = 256
SUMS = 16
TOK_DEV = 768
TOKENS = 12288
N_HEAD = 2


def shared_rows(key):
    base_rows = jnp.clip(jax.random.normal(jax.random.fold_in(key, 71), (TOKENS, H * HD), jnp.float32), -5.0, 5.0)
    return base_rows


def draw_keys(key, part):
    base_rows = shared_rows(key)
    result = base_rows
    return result.astype(jnp.bfloat16)


def draw_queries(key, part):
    key = jax.random.fold_in(key, 5)
    result = jnp.clip(1.5 * jax.random.normal(key, (TOKENS, H * HD), jnp.float32), -9.0, 9.0)
    return result.astype(jnp.bfloat16)


def raised(values, key, source, target, shards_of, factor):
    def block_of(axis_at):
        return (jnp.arange(values.shape[axis_at]) // (values.shape[axis_at] // shards_of)).reshape((-1,) + (1,) * (values.ndim - 1 - axis_at))

    near = jax.random.permutation(key, shards_of)[block_of(target)]
    far = (block_of(target) + shards_of // 2) % shards_of
    return jnp.where((block_of(source) == near) | (block_of(source) == far), factor * values, values)


def block_scale(key, shape, split, least, high):
    factor_of, own = 1.0, jax.random.fold_in(key, 6)
    for position, shards_of in split:
        heights = jnp.exp(jax.random.uniform(jax.random.fold_in(own, position), (shards_of,), jnp.float32, least / len(split), high / len(split)))
        factor_of = factor_of * jnp.repeat(heights, shape[position] // shards_of).reshape([-1 if axis == position else 1 for axis in range(len(shape))])
    return factor_of


def noise(key, extent, deviation, reach, cuts=(), kind=jnp.bfloat16):
    entries = deviation * jax.random.normal(key, extent, jnp.float32)
    if cuts:
        entries = entries * block_scale(key, extent, cuts, -0.22, 0.18)
    return jnp.clip(entries, -reach, reach).astype(kind)


def noise_with(rng, shape, spread, reach, shards, heavy, held_as=jnp.bfloat16):
    entries = spread * jax.random.normal(rng, shape, jnp.float32)
    if shards:
        entries = entries * block_scale(rng, shape, shards, -0.22, 0.18)
    return jnp.clip(raised(entries, jax.random.fold_in(rng, 3), *heavy), -reach, reach).astype(held_as)


def setup_inputs(seed: int = 0) -> dict:
    seeds = jax.random.split(jax.random.key(seed), 5)
    queries = draw_queries(jax.random.fold_in(seeds[4], 71), 0)
    keys = draw_keys(jax.random.fold_in(seeds[4], 71), 0)
    values = noise(seeds[2], (TOKENS, H * HD), 1.0, 6.0, ((0, 16), (1, 2)))
    w_out = noise_with(seeds[3], (H * HD, D), 0.125, 2.5, ((0, 2),), (0, 1, 2, 2.0))
    return dict(queries=queries, keys=keys, values=values, w_out=w_out)


NEG_FILL = -1e+30

def reference(queries, keys, values, w_out):
    feat_width = H * HD
    score_scale = 1.0 / math.sqrt(HD)
    sum_rows = TOKENS // BLOCK * SUMS
    key_sums = keys.reshape(TOKENS // BLOCK, BLOCK, feat_width)[:, BLOCK - SUMS:, :].reshape(sum_rows, feat_width)
    value_sums = values.reshape(TOKENS // BLOCK, BLOCK, feat_width)[:, BLOCK - SUMS:, :].reshape(sum_rows, feat_width)
    sum_index = jnp.arange(sum_rows, dtype=jnp.int32)
    sum_pos = sum_index // SUMS * BLOCK + BLOCK - SUMS + sum_index % SUMS
    key_padded = jnp.concatenate([jnp.zeros((BLOCK, feat_width), jnp.bfloat16), keys], axis=0)
    value_padded = jnp.concatenate([jnp.zeros((BLOCK, feat_width), jnp.bfloat16), values], axis=0)

    def one_block(block_id):
        row_start = (block_id * TOK_DEV).astype(jnp.int32)
        query_rows = lax.dynamic_slice_in_dim(queries, row_start, TOK_DEV, 0)
        band_keys = lax.dynamic_slice_in_dim(key_padded, row_start, TOK_DEV + BLOCK, 0)
        band_values = lax.dynamic_slice_in_dim(value_padded, row_start, TOK_DEV + BLOCK, 0)
        query_pos = row_start + jnp.arange(TOK_DEV, dtype=jnp.int32)
        key_pos = row_start - BLOCK + jnp.arange(TOK_DEV + BLOCK, dtype=jnp.int32)
        band_ok = (key_pos[None, :] <= query_pos[:, None]) & (key_pos[None, :] > query_pos[:, None] - BLOCK)
        sum_ok = sum_pos[None, :] <= query_pos[:, None] - BLOCK
        allowed = jnp.concatenate([band_ok, sum_ok], axis=1)
        all_keys = jnp.concatenate([band_keys, key_sums], axis=0).reshape(-1, H, HD).astype(jnp.float32)
        all_values = jnp.concatenate([band_values, value_sums], axis=0).reshape(-1, H, HD).astype(jnp.float32)
        query_heads = query_rows.reshape(TOK_DEV, H, HD).astype(jnp.float32)
        score = jnp.einsum('qhd,khd->hqk', query_heads, all_keys) * score_scale
        score = jnp.where(allowed[None], score, NEG_FILL)
        row_max = lax.optimization_barrier(jnp.max(score, axis=-1, keepdims=True))
        expo = jnp.where(allowed[None], jnp.exp(score - row_max), 0.0)
        total = lax.optimization_barrier(jnp.sum(expo, axis=-1, keepdims=True))
        weights = (expo / total).astype(jnp.bfloat16)
        attended = jnp.einsum('hqk,khd->qhd', weights.astype(jnp.float32), all_values)
        return attended.astype(jnp.bfloat16).reshape(TOK_DEV, feat_width)
    attended = lax.map(one_block, jnp.arange(TOKENS // TOK_DEV, dtype=jnp.int32)).reshape(TOKENS, feat_width)
    group_width = feat_width // N_HEAD
    summed = jnp.zeros((TOKENS, D), jnp.float32)
    for group in range(N_HEAD):
        partial_term = jnp.dot(attended[:, group * group_width:(group + 1) * group_width], w_out[group * group_width:(group + 1) * group_width, :], preferred_element_type=jnp.float32).astype(jnp.bfloat16)
        partial_term = lax.optimization_barrier(partial_term)
        summed = summed + partial_term.astype(jnp.float32)
    return summed.astype(jnp.bfloat16)
```

```python
import functools
import math

import jax
import jax.numpy as jnp
from jax import lax
from jax.experimental import pallas as pl
from jax.experimental.pallas import tpu as pltpu
from jax.sharding import PartitionSpec as P

HD = 128
BLOCK = 256
SUMS = 16
NEG = -3.3e38
SCALE2 = math.log2(math.e) / math.sqrt(HD)


def attend_kernel(pieces, info_ref, q_ref, kp_ref, vp_ref, k_ref, v_ref, bias_ref, *rest):
    sums, out_ref = rest[:pieces], rest[pieces]
    q = q_ref[...]
    nt = (((1,), (1,)), ((), ()))
    per = sums[0].shape[0] // 2
    k_sum = jnp.concatenate([s[0:per, :] for s in sums], axis=0)
    v_sum = jnp.concatenate([s[per : 2 * per, :] for s in sums], axis=0)

    def score(keys):
        return lax.dot_general(q, keys, nt, preferred_element_type=jnp.float32) * SCALE2

    row = lax.broadcasted_iota(jnp.int32, (BLOCK, BLOCK), 0)
    col = lax.broadcasted_iota(jnp.int32, (BLOCK, BLOCK), 1)
    s_prev = jnp.where((col > row) | (col >= info_ref[0]), score(kp_ref[...]), NEG)
    s_own = jnp.where(col <= row, score(k_ref[...]), NEG)
    s_sum = jnp.where(bias_ref[...] >= 0.0, score(k_sum), NEG)
    top = jnp.maximum(
        jnp.maximum(jnp.max(s_prev, axis=1, keepdims=True), jnp.max(s_own, axis=1, keepdims=True)),
        jnp.max(s_sum, axis=1, keepdims=True),
    )
    total = jnp.zeros((BLOCK, 1), jnp.float32)
    mixed = jnp.zeros((BLOCK, HD), jnp.float32)
    for s, vals in ((s_prev, vp_ref[...]), (s_own, v_ref[...]), (s_sum, v_sum)):
        e = jnp.exp2(s - top)
        total = total + jnp.sum(e, axis=1, keepdims=True)
        mixed = mixed + jnp.dot(e.astype(jnp.bfloat16), vals, preferred_element_type=jnp.float32)
    out_ref[...] = (mixed / total).astype(jnp.bfloat16)


def attend(block, info, bias, queries, keys, values, prev_k, prev_v, prev_block, sums):
    width = queries.shape[1]
    heads = width // HD
    own = pl.BlockSpec((BLOCK, HD), lambda h: (block, h))
    prev = pl.BlockSpec((BLOCK, HD), lambda h: (prev_block, h))
    sum_rows = sums[0].shape[0]
    piece = pl.BlockSpec((sum_rows, HD), lambda h: (0, h))
    n_keys = 2 * BLOCK + bias.shape[1]
    return pl.pallas_call(
        functools.partial(attend_kernel, len(sums)),
        grid=(heads,),
        in_specs=[
            pl.BlockSpec(memory_space=pltpu.SMEM),
            own,
            prev,
            prev,
            own,
            own,
            pl.BlockSpec((1, bias.shape[1]), lambda h: (0, 0)),
        ]
        + [piece] * len(sums),
        out_specs=pl.BlockSpec((BLOCK, HD), lambda h: (0, h)),
        out_shape=jax.ShapeDtypeStruct((BLOCK, width), jnp.bfloat16),
        compiler_params=pltpu.CompilerParams(vmem_limit_bytes=48 * 1024 * 1024),
        cost_estimate=pl.CostEstimate(
            flops=heads * BLOCK * n_keys * HD * 4,
            bytes_accessed=4 * width * (2 * BLOCK + bias.shape[1]),
            transcendentals=heads * BLOCK * n_keys,
        ),
    )(info, queries, prev_k, prev_v, keys, values, bias, *sums)


def gather_sums(own, count):
    me = lax.axis_index("ctx")
    if count != 16:
        rows = own.shape[0]
        whole = lax.all_gather(own, "ctx", axis=0, tiled=True)
        return [whole[i * rows : (i + 1) * rows] for i in range(count)], [jnp.int32(i) for i in range(count)]

    def up(value, steps):
        return lax.ppermute(value, "ctx", [(i, i + steps) for i in range(count - steps)])

    def flip(value, bit):
        return lax.ppermute(value, "ctx", [(i, i ^ bit) for i in range(count)])

    pieces = [own] + [up(own, 4 * k) for k in (1, 2, 3)]
    source = [me - 4 * k for k in range(4)]
    for bit in (2, 1):
        pieces = pieces + [flip(p, bit) for p in pieces]
        near = jnp.where((me & bit) != 0, -bit, bit)
        source = source + [s + near for s in source]
    return pieces, source


def per_device(n_ctx, n_head, queries, keys, values, w_out):
    rows, width = queries.shape
    blocks = rows // BLOCK
    me = lax.axis_index("ctx")
    side = lax.axis_index("head")
    ends = [slice(b * BLOCK + BLOCK - SUMS, (b + 1) * BLOCK) for b in range(blocks)]
    own = jnp.concatenate([keys[e] for e in ends] + [values[e] for e in ends], axis=0)
    sums, source = gather_sums(own, n_ctx)

    tail = jnp.concatenate([keys[rows - BLOCK :], values[rows - BLOCK :]], axis=0)
    tail, held = lax.optimization_barrier((tail, sums[len(sums) // 2 - 1]))
    sums[len(sums) // 2 - 1] = held
    rim = lax.ppermute(tail, "ctx", [(i, i + 1) for i in range(n_ctx - 1)])

    source_block = (
        jnp.stack(source)[:, None, None] * blocks + jnp.arange(blocks, dtype=jnp.int32)[None, :, None]
    )
    source_block = jnp.broadcast_to(source_block, (len(source), blocks, SUMS)).reshape(1, -1)
    present = source_block >= 0

    out_width = w_out.shape[1] // n_head
    out_parts = [None] * blocks
    for b in list(range(1, blocks)) + [0]:
        bias = jnp.where(present & (source_block <= me * blocks + b - 2), 0.0, NEG).astype(jnp.float32)
        if b == 0:
            info = jnp.where(me == 0, BLOCK, BLOCK - SUMS).astype(jnp.int32).reshape(1)
            att = attend(0, info, bias, queries, keys, values, rim[:BLOCK], rim[BLOCK:], 0, sums)
        else:
            info = jnp.full((1,), BLOCK - SUMS, jnp.int32)
            att = attend(b, info, bias, queries, keys, values, keys, values, b - 1, sums)

        def partial(step):
            at = lax.rem(side + step, n_head) * out_width
            w = lax.dynamic_slice_in_dim(w_out, at, out_width, 1)
            return jnp.dot(att, w, preferred_element_type=jnp.float32).astype(jnp.bfloat16)

        got = [
            lax.ppermute(partial(step), "head", [(i, (i + step) % n_head) for i in range(n_head)])
            for step in range(1, n_head)
        ]
        total = partial(0).astype(jnp.float32)
        for g in got:
            total = total + g.astype(jnp.float32)
        out_parts[b] = total.astype(jnp.bfloat16)
    return jnp.concatenate(out_parts, axis=0)


def solution(mesh):
    in_specs = (P("ctx", "head"), P("ctx", "head"), P("ctx", "head"), P("head", None))
    return jax.shard_map(
        functools.partial(per_device, mesh.shape["ctx"], mesh.shape["head"]),
        mesh=mesh,
        in_specs=in_specs,
        out_specs=P("ctx", "head"),
        check_vma=False,
    )
```

```python
import functools
import math

import jax
import jax.numpy as jnp
from jax import lax
from jax.experimental import pallas as pl
from jax.experimental.pallas import tpu as pltpu
from jax.sharding import PartitionSpec as P

HD = 128
BLOCK = 256
SUMS = 16
NEG = -3.3e38
SCALE2 = math.log2(math.e) / math.sqrt(HD)
MIB = 1024 * 1024
GROUP = 4


def copy_rows_kernel(*refs):
    out_ref, at = refs[-1], 0
    for ref in refs[:-1]:
        out_ref[at : at + ref.shape[0], :] = ref[...]
        at += ref.shape[0]


def copy_rows(parts, limit):
    width = parts[0][0].shape[1]
    total = sum(rows for _, rows, _ in parts)
    return pl.pallas_call(
        copy_rows_kernel,
        grid=(1,),
        in_specs=[pl.BlockSpec((rows, width), lambda i, at=at: (at, 0)) for _, rows, at in parts],
        out_specs=pl.BlockSpec((total, width), lambda i: (0, 0)),
        out_shape=jax.ShapeDtypeStruct((total, width), jnp.bfloat16),
        compiler_params=pltpu.CompilerParams(vmem_limit_bytes=limit),
        cost_estimate=pl.CostEstimate(flops=0, bytes_accessed=4 * total * width, transcendentals=0),
    )(*[array for array, _, _ in parts])


def source_of(key, me):
    if isinstance(key, int):
        return jnp.int32(key)
    up, flip_y, flip_core = key
    source = me - 4 * up
    for bit, flipped in ((2, flip_y), (1, flip_core)):
        if flipped:
            source = source + jnp.where((me & bit) != 0, -bit, bit)
    return source


def attend_kernel(cfg, *refs):
    blocks, block, first, keys_of, band, carried, finish = cfg
    refs = list(refs)
    q_ref = refs.pop(0)
    band_refs = [refs.pop(0) for _ in range(4 if band else 0)]
    sums = [refs.pop(0) for _ in keys_of]
    state = [refs.pop(0) for _ in range(2 if carried else 0)]
    rows, width = q_ref.shape
    me = lax.axis_index("ctx")
    if finish:
        (out_ref,) = refs
    else:
        acc_ref, stat_ref = refs

    per = sums[0].shape[0] // 2
    n_sum = len(sums) * per
    sum_col = lax.broadcasted_iota(jnp.int32, (1, n_sum), 1)
    end = jnp.zeros((1, n_sum), jnp.int32)
    for i, key in enumerate(keys_of):
        source = source_of(key, me)
        count = jnp.clip(SUMS * (blocks * (me - source) + block - 1), 0, per)
        count = jnp.where(source < 0, 0, count)
        end = jnp.where(sum_col >= i * per, i * per + count, end)
    allowed = [sum_col < end]
    if band:
        row = first + lax.broadcasted_iota(jnp.int32, (rows, BLOCK), 0)
        col = lax.broadcasted_iota(jnp.int32, (rows, BLOCK), 1)
        tail = BLOCK - SUMS
        if block == 0:
            tail = jnp.where(me == 0, BLOCK, tail)
        low, high = first // HD * HD, first + rows
        allowed = [((col > row) | (col >= tail))[:, low:], (col <= row)[:, :high]] + allowed
        cuts = [slice(low, BLOCK), slice(0, high)]
    else:
        cuts = []
    nt = (((1,), (1,)), ((), ()))
    lane = lax.broadcasted_iota(jnp.int32, (rows, HD), 1)
    stats = jnp.zeros((rows, HD), jnp.float32)

    for j in range(width // HD):
        c = slice(j * HD, (j + 1) * HD)
        q = q_ref[:, c]
        keys = [r[cut, c] for r, cut in zip(band_refs[0::2], cuts)] + [jnp.concatenate([s[0:per, c] for s in sums], axis=0)]
        vals = [r[cut, c] for r, cut in zip(band_refs[1::2], cuts)] + [s[per : 2 * per, c] for s in sums]
        score = jnp.concatenate(
            [
                jnp.where(ok, lax.dot_general(q, k, nt, preferred_element_type=jnp.float32) * SCALE2, NEG)
                for ok, k in zip(allowed, keys)
            ],
            axis=1,
        )
        top = jnp.max(score, axis=1, keepdims=True)
        if carried:
            old_top, old_total = state[1][:, j : j + 1], state[1][:, 8 + j : 9 + j]
            top = jnp.maximum(top, old_top)
        weight = jnp.exp2(score - top).astype(jnp.bfloat16)
        vals = jnp.concatenate(vals, axis=0)
        vals = jnp.concatenate([vals, jnp.ones_like(vals)], axis=1)
        mixed = jnp.dot(weight, vals, preferred_element_type=jnp.float32)
        mixed, total = mixed[:, :HD], mixed[:, HD:]
        if carried:
            keep = jnp.exp2(old_top - top)
            mixed = mixed + keep * state[0][:, c]
            total = total + keep * old_total
        if finish:
            out_ref[:, c] = (mixed / total).astype(jnp.bfloat16)
        else:
            acc_ref[:, c] = mixed
            stats = jnp.where(lane == j, top, jnp.where(lane == 8 + j, total, stats))
    if not finish:
        stat_ref[...] = stats


def attend(block, first, rows, queries, pieces, band=None, state=None, finish=True):
    width = queries.shape[1]
    part = min(width, GROUP * HD)
    steps = width // part
    blocks = queries.shape[0] // BLOCK
    at_row = (block * BLOCK + first) // rows
    operands, specs = [queries], [pl.BlockSpec((rows, part), lambda h: (at_row, h))]
    for array, at in band or []:
        operands.append(array)
        specs.append(pl.BlockSpec((BLOCK, part), lambda h, at=at: (at, h)))
    for piece in pieces.values():
        operands.append(piece)
        specs.append(pl.BlockSpec((piece.shape[0], part), lambda h: (0, h)))
    acc_spec = pl.BlockSpec((rows, part), lambda h: (0, h))
    stat_spec = pl.BlockSpec((rows, HD), lambda h: (0, h))
    if state is not None:
        operands += state
        specs += [acc_spec, stat_spec]
    if finish:
        out_specs = acc_spec
        out_shape = jax.ShapeDtypeStruct((rows, width), jnp.bfloat16)
    else:
        out_specs = [acc_spec, stat_spec]
        out_shape = [jax.ShapeDtypeStruct((rows, n), jnp.float32) for n in (width, steps * HD)]
    n_keys = (2 * BLOCK if band else 0) + sum(p.shape[0] for p in pieces.values()) // 2
    cfg = (blocks, block, first, tuple(pieces), band is not None, state is not None, finish)
    return pl.pallas_call(
        functools.partial(attend_kernel, cfg),
        grid=(steps,),
        in_specs=specs,
        out_specs=out_specs,
        out_shape=out_shape,
        compiler_params=pltpu.CompilerParams(vmem_limit_bytes=50 * MIB),
        cost_estimate=pl.CostEstimate(
            flops=width * rows * n_keys * 4,
            bytes_accessed=4 * width * n_keys,
            transcendentals=width // HD * rows * n_keys,
        ),
    )(*operands)


def add_kernel(n_parts, *refs):
    total = refs[0][...].astype(jnp.float32)
    for ref in refs[1:n_parts]:
        total = total + ref[...].astype(jnp.float32)
    refs[-1][...] = total.astype(jnp.bfloat16)


def add_into(out, rows_total, at, parts):
    rows, width = parts[0].shape
    part = pl.BlockSpec((rows, width), lambda i: (0, 0))
    extra = [] if out is None else [out]
    return pl.pallas_call(
        functools.partial(add_kernel, len(parts)),
        grid=(1,),
        in_specs=[part] * len(parts) + [pl.BlockSpec(memory_space=pl.ANY)] * len(extra),
        out_specs=pl.BlockSpec((rows, width), lambda i: (at // rows, 0)),
        out_shape=jax.ShapeDtypeStruct((rows_total, width), jnp.bfloat16),
        input_output_aliases={len(parts): 0} if extra else {},
        compiler_params=pltpu.CompilerParams(vmem_limit_bytes=8 * MIB),
        cost_estimate=pl.CostEstimate(flops=0, bytes_accessed=8 * rows * width, transcendentals=0),
    )(*parts, *extra)


def per_device(n_ctx, n_head, queries, keys, values, w_out):
    rows = queries.shape[0]
    blocks = rows // BLOCK
    side = lax.axis_index("head")
    ends = [BLOCK // SUMS * (b + 1) - 1 for b in range(blocks)]
    own = copy_rows([(a, SUMS, e) for a in (keys, values) for e in ends], 61 * MIB)
    tie = lax.optimization_barrier

    def band_of(b):
        return [(keys, b - 1), (values, b - 1), (keys, b), (values, b)]

    def tail_rows(k, v):
        return copy_rows([(a, BLOCK, blocks - 1) for a in (k, v)], 8 * MIB)

    early = {}
    states = {b: None for b in range(blocks)}
    if n_ctx != 16:
        whole = lax.all_gather(own, "ctx", axis=0, tiled=True)
        size = own.shape[0]
        late = {i: whole[i * size : (i + 1) * size] for i in range(n_ctx)}
        tail = tail_rows(keys, values)
    else:

        def send(value, pairs):
            return lax.ppermute(value, "ctx", pairs)

        def up(value, least):
            return send(value, [(i, i + 4) for i in range(4 * least - 4, n_ctx - 4)])

        def flip(value, bit):
            return send(value, [(i, i ^ bit) for i in range(n_ctx)])

        z1, y0 = up(own, 1), flip(own, 2)
        far = send(own, [(i, (i + 12) ^ 2) for i in range(4)])
        z1, y0 = tie((z1, y0))
        z2, y1 = up(z1, 2), flip(z1, 2)
        z2, y1, tail = tie((z2, y1, tail_rows(keys, values)))
        z3, y2 = up(z2, 3), flip(z2, 2)
        z3, tail = tie((z3, tail))
        early = {(0, 0, 0): own, (1, 0, 0): z1, (0, 1, 0): y0}
        early |= {(k, y, 1): flip(p, 1) for (k, y, _), p in list(early.items())}
        late = {(2, 0, 0): z2, (1, 1, 0): y1, (3, 0, 0): z3, (2, 1, 0): y2, (3, 1, 0): far}
        late |= {(k, y, 1): flip(p, 1) for (k, y, _), p in list(late.items())}

    rim = lax.ppermute(tail, "ctx", [(i, i + 1) for i in range(n_ctx - 1)])
    half = BLOCK // 2
    chunks = [(1, 0, half), (1, half, half)] + [(b, 0, BLOCK) for b in range(2, blocks)] + [(0, 0, BLOCK)]
    sent, kept, parts = [], [], []
    out_width = w_out.shape[1] // n_head
    for b, first, count in chunks:
        if len(parts) > 1:
            queries, parts[-2], _ = tie((queries, parts[-2], sent[-1]))
        elif parts:
            queries, _ = tie((queries, sent[-1]))
        if states[b] is not None:
            att = attend(b, first, count, queries, late, state=states[b])
        else:
            band = band_of(b) if b else [(rim, 0), (rim, 1), (keys, 0), (values, 0)]
            att = attend(b, first, count, queries, early | late, band=band)

        def partial(step):
            at = lax.rem(side + step, n_head) * out_width
            w = lax.dynamic_slice_in_dim(w_out, at, out_width, 1)
            return jnp.dot(att, w, preferred_element_type=jnp.float32).astype(jnp.bfloat16)

        sent.append([partial(step) for step in range(1, n_head)])
        kept.append(partial(0))
        parts.append(
            [
                lax.ppermute(value, "head", [(i, (i + step) % n_head) for i in range(n_head)])
                for step, value in enumerate(sent[-1], 1)
            ]
        )
    kept, _ = tie((kept, sent[-1]))
    out = None
    for (b, first, count), received, own_part in zip(chunks, parts, kept):
        out = add_into(out, rows, b * BLOCK + first, received + [own_part])
    return out


def solution(mesh):
    in_specs = (P("ctx", "head"), P("ctx", "head"), P("ctx", "head"), P("head", None))
    return jax.shard_map(
        functools.partial(per_device, mesh.shape["ctx"], mesh.shape["head"]),
        mesh=mesh,
        in_specs=in_specs,
        out_specs=P("ctx", "head"),
        check_vma=False,
    )
```

```python
import functools
import math

import jax
import jax.numpy as jnp
from jax import lax
from jax.experimental import pallas as pl
from jax.experimental.pallas import tpu as pltpu
from jax.sharding import PartitionSpec as P

HD = 128
BLOCK = 256
SUMS = 16
NEG = -3.3e38
SCALE2 = math.log2(math.e) / math.sqrt(HD)
MIB = 1024 * 1024
GROUP = 4


def copy_rows_kernel(*refs):
    out_ref, at = refs[-1], 0
    for ref in refs[:-1]:
        out_ref[at : at + ref.shape[0], :] = ref[...]
        at += ref.shape[0]


def copy_rows(parts, limit):
    width = parts[0][0].shape[1]
    total = sum(rows for _, rows, _ in parts)
    return pl.pallas_call(
        copy_rows_kernel,
        grid=(1,),
        in_specs=[pl.BlockSpec((rows, width), lambda i, at=at: (at, 0)) for _, rows, at in parts],
        out_specs=pl.BlockSpec((total, width), lambda i: (0, 0)),
        out_shape=jax.ShapeDtypeStruct((total, width), jnp.bfloat16),
        compiler_params=pltpu.CompilerParams(vmem_limit_bytes=limit),
        cost_estimate=pl.CostEstimate(flops=0, bytes_accessed=4 * total * width, transcendentals=0),
    )(*[array for array, _, _ in parts])


def source_of(key, me):
    if isinstance(key, int):
        return jnp.int32(key)
    up, flip_y, flip_core = key
    source = me - 4 * up
    for bit, flipped in ((2, flip_y), (1, flip_core)):
        if flipped:
            source = source + jnp.where((me & bit) != 0, -bit, bit)
    return source


def attend_kernel(cfg, *refs):
    blocks, block, first, keys_of, band, carried, finish = cfg
    refs = list(refs)
    q_ref = refs.pop(0)
    band_refs = [refs.pop(0) for _ in range(4 if band else 0)]
    sums = [refs.pop(0) for _ in keys_of]
    state = [refs.pop(0) for _ in range(2 if carried else 0)]
    rows, width = q_ref.shape
    me = lax.axis_index("ctx")
    if finish:
        (out_ref,) = refs
    else:
        acc_ref, stat_ref = refs

    per = sums[0].shape[0] // 2
    n_sum = len(sums) * per
    sum_col = lax.broadcasted_iota(jnp.int32, (1, n_sum), 1)
    end = jnp.zeros((1, n_sum), jnp.int32)
    for i, key in enumerate(keys_of):
        source = source_of(key, me)
        count = jnp.clip(SUMS * (blocks * (me - source) + block - 1), 0, per)
        count = jnp.where(source < 0, 0, count)
        end = jnp.where(sum_col >= i * per, i * per + count, end)
    allowed = [sum_col < end]
    if band:
        row = first + lax.broadcasted_iota(jnp.int32, (rows, BLOCK), 0)
        col = lax.broadcasted_iota(jnp.int32, (rows, BLOCK), 1)
        tail = BLOCK - SUMS
        if block == 0:
            tail = jnp.where(me == 0, BLOCK, tail)
        low, high = first // HD * HD, first + rows
        allowed = [((col > row) | (col >= tail))[:, low:], (col <= row)[:, :high]] + allowed
        cuts = [slice(low, BLOCK), slice(0, high)]
    else:
        cuts = []
    nt = (((1,), (1,)), ((), ()))
    lane = lax.broadcasted_iota(jnp.int32, (rows, HD), 1)
    stats = jnp.zeros((rows, HD), jnp.float32)

    for j in range(width // HD):
        c = slice(j * HD, (j + 1) * HD)
        q = q_ref[:, c]
        keys = [r[cut, c] for r, cut in zip(band_refs[0::2], cuts)] + [jnp.concatenate([s[0:per, c] for s in sums], axis=0)]
        vals = [r[cut, c] for r, cut in zip(band_refs[1::2], cuts)] + [s[per : 2 * per, c] for s in sums]
        score = jnp.concatenate(
            [
                jnp.where(ok, lax.dot_general(q, k, nt, preferred_element_type=jnp.float32) * SCALE2, NEG)
                for ok, k in zip(allowed, keys)
            ],
            axis=1,
        )
        top = jnp.max(score, axis=1, keepdims=True)
        if carried:
            old_top, old_total = state[1][:, j : j + 1], state[1][:, 8 + j : 9 + j]
            top = jnp.maximum(top, old_top)
        weight = jnp.exp2(score - top).astype(jnp.bfloat16)
        vals = jnp.concatenate(vals, axis=0)
        vals = jnp.concatenate([vals, jnp.ones_like(vals)], axis=1)
        mixed = jnp.dot(weight, vals, preferred_element_type=jnp.float32)
        mixed, total = mixed[:, :HD], mixed[:, HD:]
        if carried:
            keep = jnp.exp2(old_top - top)
            mixed = mixed + keep * state[0][:, c]
            total = total + keep * old_total
        if finish:
            out_ref[:, c] = (mixed / total).astype(jnp.bfloat16)
        else:
            acc_ref[:, c] = mixed
            stats = jnp.where(lane == j, top, jnp.where(lane == 8 + j, total, stats))
    if not finish:
        stat_ref[...] = stats


def attend(block, first, rows, queries, pieces, band=None, state=None, finish=True):
    width = queries.shape[1]
    part = min(width, GROUP * HD)
    steps = width // part
    blocks = queries.shape[0] // BLOCK
    at_row = (block * BLOCK + first) // rows
    operands, specs = [queries], [pl.BlockSpec((rows, part), lambda h: (at_row, h))]
    for array, at in band or []:
        operands.append(array)
        specs.append(pl.BlockSpec((BLOCK, part), lambda h, at=at: (at, h)))
    for piece in pieces.values():
        operands.append(piece)
        specs.append(pl.BlockSpec((piece.shape[0], part), lambda h: (0, h)))
    acc_spec = pl.BlockSpec((rows, part), lambda h: (0, h))
    stat_spec = pl.BlockSpec((rows, HD), lambda h: (0, h))
    if state is not None:
        operands += state
        specs += [acc_spec, stat_spec]
    if finish:
        out_specs = acc_spec
        out_shape = jax.ShapeDtypeStruct((rows, width), jnp.bfloat16)
    else:
        out_specs = [acc_spec, stat_spec]
        out_shape = [jax.ShapeDtypeStruct((rows, n), jnp.float32) for n in (width, steps * HD)]
    n_keys = (2 * BLOCK if band else 0) + sum(p.shape[0] for p in pieces.values()) // 2
    cfg = (blocks, block, first, tuple(pieces), band is not None, state is not None, finish)
    return pl.pallas_call(
        functools.partial(attend_kernel, cfg),
        grid=(steps,),
        in_specs=specs,
        out_specs=out_specs,
        out_shape=out_shape,
        compiler_params=pltpu.CompilerParams(vmem_limit_bytes=50 * MIB),
        cost_estimate=pl.CostEstimate(
            flops=width * rows * n_keys * 4,
            bytes_accessed=4 * width * n_keys,
            transcendentals=width // HD * rows * n_keys,
        ),
    )(*operands)


def add_kernel(n_parts, *refs):
    total = refs[0][...].astype(jnp.float32)
    for ref in refs[1:n_parts]:
        total = total + ref[...].astype(jnp.float32)
    refs[-1][...] = total.astype(jnp.bfloat16)


def add_into(out, rows_total, at, parts):
    rows, width = parts[0].shape
    part = pl.BlockSpec((rows, width), lambda i: (0, 0))
    extra = [] if out is None else [out]
    return pl.pallas_call(
        functools.partial(add_kernel, len(parts)),
        grid=(1,),
        in_specs=[part] * len(parts) + [pl.BlockSpec(memory_space=pl.ANY)] * len(extra),
        out_specs=pl.BlockSpec((rows, width), lambda i: (at // rows, 0)),
        out_shape=jax.ShapeDtypeStruct((rows_total, width), jnp.bfloat16),
        input_output_aliases={len(parts): 0} if extra else {},
        compiler_params=pltpu.CompilerParams(vmem_limit_bytes=8 * MIB),
        cost_estimate=pl.CostEstimate(flops=0, bytes_accessed=8 * rows * width, transcendentals=0),
    )(*parts, *extra)


def per_device(n_ctx, n_head, queries, keys, values, w_out):
    rows = queries.shape[0]
    blocks = rows // BLOCK
    side = lax.axis_index("head")
    ends = [BLOCK // SUMS * (b + 1) - 1 for b in range(blocks)]
    own = copy_rows([(a, SUMS, e) for a in (keys, values) for e in ends], 61 * MIB)
    tie = lax.optimization_barrier

    def band_of(b):
        return [(keys, b - 1), (values, b - 1), (keys, b), (values, b)]

    def tail_rows(k, v):
        return copy_rows([(a, BLOCK, blocks - 1) for a in (k, v)], 8 * MIB)

    early = {}
    states = {b: None for b in range(blocks)}
    if n_ctx != 16:
        whole = lax.all_gather(own, "ctx", axis=0, tiled=True)
        size = own.shape[0]
        late = {i: whole[i * size : (i + 1) * size] for i in range(n_ctx)}
        tail = tail_rows(keys, values)
    else:

        def send(value, pairs):
            return lax.ppermute(value, "ctx", pairs)

        def up(value, least):
            return send(value, [(i, i + 4) for i in range(4 * least - 4, n_ctx - 4)])

        def flip(value, bit):
            return send(value, [(i, i ^ bit) for i in range(n_ctx)])

        z1, y0 = up(own, 1), flip(own, 2)
        far = send(own, [(i, (i + 12) ^ 2) for i in range(4)])
        z1, y0 = tie((z1, y0))
        z2, y1 = up(z1, 2), flip(z1, 2)
        z2, y1, tail = tie((z2, y1, tail_rows(keys, values)))
        z3, y2 = up(z2, 3), flip(z2, 2)
        z3, tail, own, z1, y0, z2, y1 = tie((z3, tail, own, z1, y0, z2, y1))
        early = {(0, 0, 0): own, (1, 0, 0): z1, (0, 1, 0): y0}
        late = {(2, 0, 0): z2, (1, 1, 0): y1, (3, 0, 0): z3, (2, 1, 0): y2, (3, 1, 0): far}
        early |= {(k, y, 1): flip(p, 1) for (k, y, _), p in list(early.items())}
        late |= {(k, y, 1): flip(p, 1) for (k, y, _), p in list(late.items())}

    rim = lax.ppermute(tail, "ctx", [(i, i + 1) for i in range(n_ctx - 1)])
    half = BLOCK // 2
    chunks = [(1, 0, half), (1, half, half)] + [(b, 0, BLOCK) for b in range(2, blocks)] + [(0, 0, BLOCK)]
    sent, kept, parts = [], [], []
    out_width = w_out.shape[1] // n_head
    for b, first, count in chunks:
        if len(parts) > 1:
            queries, parts[-2], _ = tie((queries, parts[-2], sent[-1]))
        elif parts:
            queries, _ = tie((queries, sent[-1]))
        if states[b] is not None:
            att = attend(b, first, count, queries, late, state=states[b])
        else:
            band = band_of(b) if b else [(rim, 0), (rim, 1), (keys, 0), (values, 0)]
            att = attend(b, first, count, queries, early | late, band=band)

        def partial(step):
            at = lax.rem(side + step, n_head) * out_width
            w = lax.dynamic_slice_in_dim(w_out, at, out_width, 1)
            return jnp.dot(att, w, preferred_element_type=jnp.float32).astype(jnp.bfloat16)

        sent.append([partial(step) for step in range(1, n_head)])
        kept.append(partial(0))
        parts.append(
            [
                lax.ppermute(value, "head", [(i, (i + step) % n_head) for i in range(n_head)])
                for step, value in enumerate(sent[-1], 1)
            ]
        )
    kept, _ = tie((kept, sent[-1]))
    out = None
    for (b, first, count), received, own_part in zip(chunks, parts, kept):
        out = add_into(out, rows, b * BLOCK + first, received + [own_part])
    return out


def solution(mesh):
    in_specs = (P("ctx", "head"), P("ctx", "head"), P("ctx", "head"), P("head", None))
    return jax.shard_map(
        functools.partial(per_device, mesh.shape["ctx"], mesh.shape["head"]),
        mesh=mesh,
        in_specs=in_specs,
        out_specs=P("ctx", "head"),
        check_vma=False,
    )
```

```python
import functools
import math

import jax
import jax.numpy as jnp
from jax import lax
from jax.experimental import pallas as pl
from jax.experimental.pallas import tpu as pltpu
from jax.sharding import PartitionSpec as P

HD = 128
BLOCK = 256
SUMS = 16
NEG = -3.3e38
SCALE2 = math.log2(math.e) / math.sqrt(HD)
MIB = 1024 * 1024
GROUP = 4


def copy_rows_kernel(*refs):
    out_ref, at = refs[-1], 0
    for ref in refs[:-1]:
        out_ref[at : at + ref.shape[0], :] = ref[...]
        at += ref.shape[0]


def copy_rows(parts, limit):
    width = parts[0][0].shape[1]
    total = sum(rows for _, rows, _ in parts)
    return pl.pallas_call(
        copy_rows_kernel,
        grid=(1,),
        in_specs=[pl.BlockSpec((rows, width), lambda i, at=at: (at, 0)) for _, rows, at in parts],
        out_specs=pl.BlockSpec((total, width), lambda i: (0, 0)),
        out_shape=jax.ShapeDtypeStruct((total, width), jnp.bfloat16),
        compiler_params=pltpu.CompilerParams(vmem_limit_bytes=limit),
        cost_estimate=pl.CostEstimate(flops=0, bytes_accessed=4 * total * width, transcendentals=0),
    )(*[array for array, _, _ in parts])


def source_of(key, me):
    if isinstance(key, int):
        return jnp.int32(key)
    up, flip_y, flip_core = key
    source = me - 4 * up
    for bit, flipped in ((2, flip_y), (1, flip_core)):
        if flipped:
            source = source + jnp.where((me & bit) != 0, -bit, bit)
    return source


def attend_kernel(cfg, *refs):
    blocks, block, first, keys_of, band, carried, finish = cfg
    refs = list(refs)
    q_ref = refs.pop(0)
    band_refs = [refs.pop(0) for _ in range(4 if band else 0)]
    sums = [refs.pop(0) for _ in keys_of]
    state = [refs.pop(0) for _ in range(2 if carried else 0)]
    rows, width = q_ref.shape
    me = lax.axis_index("ctx")
    if finish:
        (out_ref,) = refs
    else:
        acc_ref, stat_ref = refs

    per = sums[0].shape[0] // 2
    n_sum = len(sums) * per
    sum_col = lax.broadcasted_iota(jnp.int32, (1, n_sum), 1)
    end = jnp.zeros((1, n_sum), jnp.int32)
    for i, key in enumerate(keys_of):
        source = source_of(key, me)
        count = jnp.clip(SUMS * (blocks * (me - source) + block - 1), 0, per)
        count = jnp.where(source < 0, 0, count)
        end = jnp.where(sum_col >= i * per, i * per + count, end)
    allowed = [sum_col < end]
    if band:
        row = first + lax.broadcasted_iota(jnp.int32, (rows, BLOCK), 0)
        col = lax.broadcasted_iota(jnp.int32, (rows, BLOCK), 1)
        tail = BLOCK - SUMS
        if block == 0:
            tail = jnp.where(me == 0, BLOCK, tail)
        low, high = first // HD * HD, first + rows
        allowed = [((col > row) | (col >= tail))[:, low:], (col <= row)[:, :high]] + allowed
        cuts = [slice(low, BLOCK), slice(0, high)]
    else:
        cuts = []
    nt = (((1,), (1,)), ((), ()))
    lane = lax.broadcasted_iota(jnp.int32, (rows, HD), 1)
    stats = jnp.zeros((rows, HD), jnp.float32)

    for j in range(width // HD):
        c = slice(j * HD, (j + 1) * HD)
        q = q_ref[:, c]
        keys = [r[cut, c] for r, cut in zip(band_refs[0::2], cuts)] + [jnp.concatenate([s[0:per, c] for s in sums], axis=0)]
        vals = [r[cut, c] for r, cut in zip(band_refs[1::2], cuts)] + [s[per : 2 * per, c] for s in sums]
        score = jnp.concatenate(
            [
                jnp.where(ok, lax.dot_general(q, k, nt, preferred_element_type=jnp.float32) * SCALE2, NEG)
                for ok, k in zip(allowed, keys)
            ],
            axis=1,
        )
        top = jnp.max(score, axis=1, keepdims=True)
        if carried:
            old_top, old_total = state[1][:, j : j + 1], state[1][:, 8 + j : 9 + j]
            top = jnp.maximum(top, old_top)
        weight = jnp.exp2(score - top).astype(jnp.bfloat16)
        vals = jnp.concatenate(vals, axis=0)
        vals = jnp.concatenate([vals, jnp.ones_like(vals)], axis=1)
        mixed = jnp.dot(weight, vals, preferred_element_type=jnp.float32)
        mixed, total = mixed[:, :HD], mixed[:, HD:]
        if carried:
            keep = jnp.exp2(old_top - top)
            mixed = mixed + keep * state[0][:, c]
            total = total + keep * old_total
        if finish:
            out_ref[:, c] = (mixed / total).astype(jnp.bfloat16)
        else:
            acc_ref[:, c] = mixed
            stats = jnp.where(lane == j, top, jnp.where(lane == 8 + j, total, stats))
    if not finish:
        stat_ref[...] = stats


def attend(block, first, rows, queries, pieces, band=None, state=None, finish=True):
    width = queries.shape[1]
    part = min(width, GROUP * HD)
    steps = width // part
    blocks = queries.shape[0] // BLOCK
    at_row = (block * BLOCK + first) // rows
    operands, specs = [queries], [pl.BlockSpec((rows, part), lambda h: (at_row, h))]
    for array, at in band or []:
        operands.append(array)
        specs.append(pl.BlockSpec((BLOCK, part), lambda h, at=at: (at, h)))
    for piece in pieces.values():
        operands.append(piece)
        specs.append(pl.BlockSpec((piece.shape[0], part), lambda h: (0, h)))
    acc_spec = pl.BlockSpec((rows, part), lambda h: (0, h))
    stat_spec = pl.BlockSpec((rows, HD), lambda h: (0, h))
    if state is not None:
        operands += state
        specs += [acc_spec, stat_spec]
    if finish:
        out_specs = acc_spec
        out_shape = jax.ShapeDtypeStruct((rows, width), jnp.bfloat16)
    else:
        out_specs = [acc_spec, stat_spec]
        out_shape = [jax.ShapeDtypeStruct((rows, n), jnp.float32) for n in (width, steps * HD)]
    n_keys = (2 * BLOCK if band else 0) + sum(p.shape[0] for p in pieces.values()) // 2
    cfg = (blocks, block, first, tuple(pieces), band is not None, state is not None, finish)
    return pl.pallas_call(
        functools.partial(attend_kernel, cfg),
        grid=(steps,),
        in_specs=specs,
        out_specs=out_specs,
        out_shape=out_shape,
        compiler_params=pltpu.CompilerParams(vmem_limit_bytes=50 * MIB),
        cost_estimate=pl.CostEstimate(
            flops=width * rows * n_keys * 4,
            bytes_accessed=4 * width * n_keys,
            transcendentals=width // HD * rows * n_keys,
        ),
    )(*operands)


def add_kernel(n_parts, *refs):
    total = refs[0][...].astype(jnp.float32)
    for ref in refs[1:n_parts]:
        total = total + ref[...].astype(jnp.float32)
    refs[-1][...] = total.astype(jnp.bfloat16)


def add_into(out, rows_total, at, parts):
    rows, width = parts[0].shape
    part = pl.BlockSpec((rows, width), lambda i: (0, 0))
    extra = [] if out is None else [out]
    return pl.pallas_call(
        functools.partial(add_kernel, len(parts)),
        grid=(1,),
        in_specs=[part] * len(parts) + [pl.BlockSpec(memory_space=pl.ANY)] * len(extra),
        out_specs=pl.BlockSpec((rows, width), lambda i: (at // rows, 0)),
        out_shape=jax.ShapeDtypeStruct((rows_total, width), jnp.bfloat16),
        input_output_aliases={len(parts): 0} if extra else {},
        compiler_params=pltpu.CompilerParams(vmem_limit_bytes=8 * MIB),
        cost_estimate=pl.CostEstimate(flops=0, bytes_accessed=8 * rows * width, transcendentals=0),
    )(*parts, *extra)


def per_device(n_ctx, n_head, queries, keys, values, w_out):
    rows = queries.shape[0]
    blocks = rows // BLOCK
    side = lax.axis_index("head")
    ends = [BLOCK // SUMS * (b + 1) - 1 for b in range(blocks)]
    own = copy_rows([(a, SUMS, e) for a in (keys, values) for e in ends], 61 * MIB)
    tie = lax.optimization_barrier

    def band_of(b):
        return [(keys, b - 1), (values, b - 1), (keys, b), (values, b)]

    def tail_rows(k, v):
        return copy_rows([(a, BLOCK, blocks - 1) for a in (k, v)], 8 * MIB)

    early = {}
    states = {b: None for b in range(blocks)}
    if n_ctx != 16:
        whole = lax.all_gather(own, "ctx", axis=0, tiled=True)
        size = own.shape[0]
        late = {i: whole[i * size : (i + 1) * size] for i in range(n_ctx)}
        tail = tail_rows(keys, values)
    else:

        def send(value, pairs):
            return lax.ppermute(value, "ctx", pairs)

        def up(value, least):
            return send(value, [(i, i + 4) for i in range(4 * least - 4, n_ctx - 4)])

        def flip(value, bit):
            return send(value, [(i, i ^ bit) for i in range(n_ctx)])

        z1, y0 = up(own, 1), flip(own, 2)
        far = send(own, [(i, (i + 12) ^ 2) for i in range(4)])
        z1, y0 = tie((z1, y0))
        z2, y1 = up(z1, 2), flip(z1, 2)
        z2, y1, tail = tie((z2, y1, tail_rows(keys, values)))
        z3, y2 = up(z2, 3), flip(z2, 2)
        y2, tail, z2, y1 = tie((y2, tail, z2, y1))
        z3, own, z1, y0 = tie((z3, own, z1, y0))
        early = {(0, 0, 0): own, (1, 0, 0): z1, (0, 1, 0): y0}
        late = {(2, 0, 0): z2, (1, 1, 0): y1, (3, 0, 0): z3, (2, 1, 0): y2, (3, 1, 0): far}
        early |= {(k, y, 1): flip(p, 1) for (k, y, _), p in list(early.items())}
        late |= {(k, y, 1): flip(p, 1) for (k, y, _), p in list(late.items())}

    rim = lax.ppermute(tail, "ctx", [(i, i + 1) for i in range(n_ctx - 1)])
    half = BLOCK // 2
    chunks = [(1, 0, half), (1, half, half)] + [(b, 0, BLOCK) for b in range(2, blocks)] + [(0, 0, BLOCK)]
    sent, kept, parts = [], [], []
    out_width = w_out.shape[1] // n_head
    for b, first, count in chunks:
        if len(parts) > 1:
            queries, parts[-2], _ = tie((queries, parts[-2], sent[-1]))
        elif parts:
            queries, _ = tie((queries, sent[-1]))
        if states[b] is not None:
            att = attend(b, first, count, queries, late, state=states[b])
        else:
            band = band_of(b) if b else [(rim, 0), (rim, 1), (keys, 0), (values, 0)]
            att = attend(b, first, count, queries, early | late, band=band)

        def partial(step):
            at = lax.rem(side + step, n_head) * out_width
            w = lax.dynamic_slice_in_dim(w_out, at, out_width, 1)
            return jnp.dot(att, w, preferred_element_type=jnp.float32).astype(jnp.bfloat16)

        sent.append([partial(step) for step in range(1, n_head)])
        kept.append(partial(0))
        parts.append(
            [
                lax.ppermute(value, "head", [(i, (i + step) % n_head) for i in range(n_head)])
                for step, value in enumerate(sent[-1], 1)
            ]
        )
    kept, _ = tie((kept, sent[-1]))
    out = None
    for (b, first, count), received, own_part in zip(chunks, parts, kept):
        out = add_into(out, rows, b * BLOCK + first, received + [own_part])
    return out


def solution(mesh):
    in_specs = (P("ctx", "head"), P("ctx", "head"), P("ctx", "head"), P("head", None))
    return jax.shard_map(
        functools.partial(per_device, mesh.shape["ctx"], mesh.shape["head"]),
        mesh=mesh,
        in_specs=in_specs,
        out_specs=P("ctx", "head"),
        check_vma=False,
    )
```
